256 devices in a mesh: blk: 128 (over z, x_lo, y, core), rep: 2 (over x_hi).
Axes of the slice: x: 4 (x_hi: 2, x_lo: 2; x = x_hi * 2 + x_lo), y: 4, z: 8, core: 2. Of those that a mesh axis runs over, the one named last changes fastest.
Arguments:
- pooled: bfloat16 [2, 16384, 1536], P('rep', 'blk'), may hold values from -6 to 6
- w_img: bfloat16 [1536, 1024], replicated, may hold values from -0.15625 to 0.15625
- text_emb: bfloat16 [2, 16384, 1024], P('rep', 'blk'), may hold values from -6 to 6
- pos_index: int32 [2, 16384], P('rep', 'blk'), may hold values from 0 to 16383, each once within a row
- log_scale: float32 [1], replicated, may hold values from 1.5 to 2.5
- bias: float32 [1], replicated, may hold values from -2 to -0.5
Outputs:
- row_loss: float32 [2, 16384], P('rep', 'blk')
- weight_grad: float32 [1536, 1024], P(('blk', 'rep'))
- text_grad: float32 [2, 16384, 1024], P('rep', 'blk')
The draws below stay inside these ranges and needn't reach their ends.
Inputs may be any that keep to these rules, and one draw needn't show every extreme that they name: `pos_index`: each group's row is a permutation of 0 to 16383.
All inputs are finite; a program needn't handle non-finite values.
Results may differ from the reference program's by a relative error of at most 0.0052.
Values may be sent and summed in bfloat16 or wider, within the bound.
No kernel may reach another device: no remote copies, remote signals or barrier semaphores. Data moves between devices by JAX's collectives and lax.ppermute only.
A program may use at most 192 MiB of HBM per device.

```python
import jax
import jax.numpy as jnp
from jax import lax

D_IMG = 1536
D_EMB = 1024
REPS = 2
BG = 16384


def level_of(own_key, extent, cuts, least, high):
    def one(dim, parts):
        draws = jax.random.uniform(jax.random.fold_in(jax.random.fold_in(own_key, 6), dim), (parts,), jnp.float32, least / len(cuts), high / len(cuts))
        return jnp.repeat(jnp.exp(draws), extent[dim] // parts).reshape((-1,) + (1,) * (len(extent) - dim - 1))

    gain = one(*cuts[0])
    for cut in cuts[1:]:
        gain = gain * one(*cut)
    return gain


def centred(stream_key, extent, spread, most, pieces=(), kind=jnp.bfloat16):
    array = jax.random.normal(stream_key, extent, jnp.float32) * spread
    if len(pieces) > 0:
        array = level_of(stream_key, extent, pieces, -0.22, 0.18) * array
    return jnp.clip(array, min=-most, max=most).astype(kind)


def setup_inputs(seed: int = 0) -> dict:
    streams_of = jax.random.split(jax.random.key(seed), 7)
    return {
        "pooled": centred(streams_of[0], (REPS, BG, D_IMG), 1.0, 6.0, ((0, 2), (1, 128))),
        "w_img": centred(streams_of[1], (D_IMG, D_EMB), D_IMG ** -0.5, 0.15625),
        "text_emb": centred(streams_of[2], (REPS, BG, D_EMB), 1.0, 6.0, ((0, 2), (1, 128))),
        "pos_index": jax.vmap(lambda own: jax.random.permutation(own, BG))(jax.random.split(streams_of[3], REPS)).reshape((REPS, BG)).astype(jnp.int32),
        "log_scale": jnp.clip(jax.random.uniform(streams_of[4], (1,), jnp.float32, 1.5, 2.5), 1.5, 2.5),
        "bias": jnp.clip(jax.random.uniform(streams_of[5], (1,), jnp.float32, -2.0, -0.5), -2.0, -0.5),
    }


def normalize(rows):
    squares = lax.optimization_barrier(jnp.sum(rows * rows, axis=-1, keepdims=True))
    inverse = lax.rsqrt(squares + 1e-06)
    return (rows * inverse, inverse)

def pair_terms(left, right, left_pos, right_start, scale_value, shift):
    logits = scale_value * jnp.dot(left, right.T, preferred_element_type=jnp.float32) + shift
    columns = right_start + jnp.arange(right.shape[0], dtype=jnp.int32)
    sign = jnp.where(left_pos[:, None] == columns[None, :], 1.0, -1.0).astype(logits.dtype)
    losses = jax.nn.softplus(-sign * logits)
    coeffs = (-sign * jax.nn.sigmoid(-sign * logits) * scale_value).astype(jnp.bfloat16)
    return (lax.optimization_barrier(jnp.sum(losses, axis=1)), coeffs)

def reference(pooled, w_img, text_emb, pos_index, log_scale, bias):
    scale_value = jnp.exp(log_scale[0])
    shift = bias[0]
    losses_all = []
    texts_all = []
    weight_total = jnp.zeros((D_IMG, D_EMB), jnp.float32)
    for group in range(REPS):
        features = pooled[group]
        projected = jnp.dot(features, w_img, preferred_element_type=jnp.float32)
        image_unit, image_inv = normalize(projected)
        image_low = image_unit.astype(jnp.bfloat16)
        text_unit, text_inv = normalize(text_emb[group].astype(jnp.float32))
        text_low = text_unit.astype(jnp.bfloat16)
        row_sums, coeffs = pair_terms(image_low, text_low, pos_index[group], 0, scale_value, shift)
        image_dir = jnp.dot(coeffs, text_low, preferred_element_type=jnp.float32)
        text_dir = jnp.dot(coeffs.T, image_low, preferred_element_type=jnp.float32)
        image_back = ((image_dir - image_unit * lax.optimization_barrier(jnp.sum(image_unit * image_dir, axis=-1, keepdims=True))) * image_inv).astype(jnp.bfloat16)
        text_back = (text_dir - text_unit * lax.optimization_barrier(jnp.sum(text_unit * text_dir, axis=-1, keepdims=True))) * text_inv
        weight_total = weight_total + jnp.dot(features.T, image_back, preferred_element_type=jnp.float32)
        losses_all.append(row_sums / BG)
        texts_all.append(text_back)
    return (jnp.stack(losses_all), weight_total / 64.0, jnp.stack(texts_all))
```

```python
import functools

import jax
import jax.numpy as jnp
from jax import lax
from jax.experimental import pallas as pl
from jax.experimental.pallas import tpu as pltpu
from jax.sharding import Mesh
from jax.sharding import PartitionSpec as P

NZ, NX, NY, NC, NR = 8, 2, 4, 2, 2
ROWS = 128
D_IMG = 1536
D_EMB = 1024
PAD = 128
IMGS = NX * NY * ROWS
TEXTS = NZ * NC * ROWS
STEP = 256
CHUNK = 512
LOG2E = 1.4426950408889634
LN2 = 0.6931471805599453
BF, F32 = jnp.bfloat16, jnp.float32


def shift(x, axis, n, by):
    return lax.ppermute(x, axis, [(i, (i + by) % n) for i in range(n)])


def shift_x(x, by):
    at = lambda i: (i % 2) * 2 + (i // 2) % 2
    return lax.ppermute(x, ("xl", "rep"), [(at(i), at((i + by) % 4)) for i in range(4)])


def shift_y(x, by):
    return shift(x, "y", NY, by)


def flip(x, axis, n, bit):
    return lax.ppermute(x, axis, [(i, i ^ bit) for i in range(n)])


def gather_z(x):
    half = x.shape[0] // 2
    down, up = [x], [x]
    for _ in range(3):
        down.append(shift(down[-1], "z", NZ, 1))
        up.append(shift(up[-1], "z", NZ, -1))
    far = [shift(down[3][:half], "z", NZ, 1), shift(up[3][half:], "z", NZ, -1)]
    return [x, down[1], up[1], down[2], up[2], down[3], up[3]] + far


Z_OFFSETS = (0, -1, 1, -2, 2, -3, 3, 4)
XY_OFFSETS = ((0, 0), (1, 0), (0, -1), (0, 1), (1, -1), (1, 1), (0, 2), (1, 2))


def gather_xy(x):
    half = x.shape[0] // 2
    mate = flip(x, "xl", NX, 1)
    below = shift(x, "y", NY, 1)
    above = shift(x, "y", NY, -1)
    mate_above = flip(above, "xl", NX, 1)
    mate_below = shift(mate, "y", NY, 1)
    far = shift(above, "y", NY, -1)
    mate_far = [
        shift(mate_below[:half], "y", NY, 1),
        shift(mate_above[half:], "y", NY, -1),
    ]
    return [x, mate, below, above, mate_below, mate_above, far] + mate_far


def sum_over_z(blocks):
    at = dict(zip(Z_OFFSETS, blocks))
    half = ROWS // 2
    send = lambda x, by: shift(x.astype(BF), "z", NZ, by).astype(F32)
    got_up = send(at[4][:half], 1)
    got_dn = send(at[4][half:], -1)
    up = jnp.concatenate([at[3][:half] + got_up, at[3][half:]])
    dn = jnp.concatenate([at[-3][:half], at[-3][half:] + got_dn])
    for o in (2, 1, 0):
        got_up = send(up, 1)
        got_dn = send(dn, -1)
        if o:
            up = at[o] + got_up
            dn = at[-o] + got_dn
    return at[0] + got_up + got_dn


def sum_over_ring4(w, move, me):
    pick = lambda i: lax.dynamic_index_in_dim(w, lax.rem(me + i, 4), 0, keepdims=False)
    total = pick(0)
    for by in (2, 1, 3):
        total = total + move(pick(by).astype(BF), by).astype(F32)
    return total


def sum_weight(w):
    core, y = lax.axis_index("core"), lax.axis_index("y")
    x = lax.axis_index("rep") * 2 + lax.axis_index("xl")
    z = lax.axis_index("z")
    mine = lax.dynamic_index_in_dim(w, core, 0, keepdims=False)
    other = lax.dynamic_index_in_dim(w, 1 - core, 0, keepdims=False)
    w = mine + flip(other.astype(BF), "core", NC, 1).astype(F32)
    half = D_EMB // 2
    a = sum_over_ring4(w[..., :half], shift_x, x)
    b = sum_over_ring4(jnp.swapaxes(w[..., half:], 0, 1), shift_y, y)
    a = sum_over_ring4(a, shift_y, y)
    b = sum_over_ring4(b, shift_x, x)
    w = jnp.concatenate([a, b], axis=1)
    rows = w.shape[0]
    for bit, kind in ((4, BF), (2, F32), (1, F32)):
        rows //= 2
        here = lax.rem(z // bit, 2)
        mine = lax.dynamic_slice_in_dim(w, here * rows, rows, 0)
        other = lax.dynamic_slice_in_dim(w, (1 - here) * rows, rows, 0)
        w = mine + flip(other.astype(kind), "z", NZ, bit).astype(F32)
    return w


def sum_losses(losses):
    at = {o: losses[i] for i, o in enumerate(XY_OFFSETS)}
    ys = (0, -1, 1, 2)
    mate = jnp.stack([at[(1, o)] for o in ys])
    mine = jnp.stack([at[(0, o)] for o in ys]) + flip(mate, "xl", NX, 1)
    total = mine[0]
    for i, o in enumerate(ys[1:]):
        total = total + shift(mine[i + 1], "y", NY, o)
    return total


NN = (((1,), (0,)), ((), ()))
NT = (((1,), (1,)), ((), ()))
TN = (((0,), (0,)), ((), ()))


def dot(a, b, dims):
    return lax.dot_general(a, b, dims, preferred_element_type=F32)


def tile_kernel(scalars, pooled, w_img, texts, columns, loss, mine, other, weight, text_sum, w_sum):
    step = pl.program_id(0)
    scale = scalars[0]
    shift_value = scalars[1]
    features = pooled[:, :D_IMG]
    codes = pooled[:, D_IMG : D_IMG + 2].astype(F32)
    positive = (codes[:, 0:1] * 128.0 + codes[:, 1:2]).astype(jnp.int32)
    projected = dot(features, w_img[...], NN)
    inverse = lax.rsqrt(jnp.sum(projected * projected, axis=1, keepdims=True) + 1e-06)
    unit = projected * inverse
    low = unit.astype(BF)

    @pl.when(step == 0)
    def _():
        text_sum[...] = jnp.zeros_like(text_sum)
        w_sum[...] = jnp.zeros_like(w_sum)

    direction = jnp.zeros((STEP, D_EMB), F32)
    logs = jnp.zeros((STEP, CHUNK), F32)
    rest = jnp.zeros((STEP, CHUNK), F32)
    for c in range(TEXTS // CHUNK):
        at = slice(c * CHUNK, (c + 1) * CHUNK)
        text = texts[at, :]
        logits = scale * dot(low, text, NT) + shift_value
        hit = positive == columns[0:1, at]
        e = jnp.exp(logits)
        u = 1.0 + e
        r = pl.reciprocal(u, approx=True)
        r = r * (2.0 - u * r)
        logs = logs + jnp.log(u)
        rest = rest + ((e - (u - 1.0)) * r - jnp.where(hit, logits, 0.0))
        share = e * r
        coeffs = (jnp.where(hit, share - 1.0, share) * scale).astype(BF)
        direction = direction + dot(coeffs, text, NN)
        text_sum[at, :] += dot(coeffs, low, TN)
    loss[...] = jnp.sum(logs + rest, axis=1, keepdims=True)
    back = (direction - unit * jnp.sum(unit * direction, axis=1, keepdims=True)) * inverse
    w_sum[...] += dot(features, back.astype(BF), TN)

    @pl.when(step == pl.num_programs(0) - 1)
    def _():
        mine[...] = text_sum[: TEXTS // 2, :]
        other[...] = text_sum[TEXTS // 2 :, :].astype(BF)
        to = 0
        for core in range(NC):
            for rep in range(NR):
                for xl in range(NX):
                    for y in range(NY):
                        for z in range(NZ):
                            frm = 6 * ((((z * NX + xl) * NY + y) * NC + core) * NR + rep)
                            weight[to : to + 6, :] = w_sum[frm : frm + 6, :]
                            to += 6


def tile(scalars, pooled, w_img, texts, columns):
    whole = lambda shape: pl.BlockSpec(shape, lambda i: (0,) * len(shape))
    return pl.pallas_call(
        tile_kernel,
        grid=(IMGS // STEP,),
        in_specs=[
            pl.BlockSpec(memory_space=pltpu.SMEM),
            pl.BlockSpec((STEP, D_IMG + PAD), lambda i: (i, 0)),
            whole((D_IMG, D_EMB)),
            whole((TEXTS, D_EMB)),
            whole((1, TEXTS)),
        ],
        out_specs=[
            pl.BlockSpec((STEP, 1), lambda i: (i, 0)),
            whole((TEXTS // 2, D_EMB)),
            whole((TEXTS // 2, D_EMB)),
            whole((D_IMG, D_EMB)),
        ],
        out_shape=[
            jax.ShapeDtypeStruct((IMGS, 1), F32),
            jax.ShapeDtypeStruct((TEXTS // 2, D_EMB), F32),
            jax.ShapeDtypeStruct((TEXTS // 2, D_EMB), BF),
            jax.ShapeDtypeStruct((D_IMG, D_EMB), F32),
        ],
        scratch_shapes=[
            pltpu.VMEM((TEXTS, D_EMB), F32),
            pltpu.VMEM((D_IMG, D_EMB), F32),
        ],
        compiler_params=pltpu.CompilerParams(vmem_limit_bytes=60 * 2**20),
        cost_estimate=pl.CostEstimate(
            flops=2 * IMGS * D_EMB * (3 * TEXTS + 2 * D_IMG),
            bytes_accessed=32 * 2**20,
            transcendentals=3 * IMGS * TEXTS,
        ),
    )(scalars, pooled, w_img, texts, columns)


def shards(pooled, w_img, text_emb, pos_index, log_scale, bias):
    scalars = jnp.stack([jnp.exp(log_scale[0]), bias[0]])
    pos = pos_index[0]
    lane = lax.broadcasted_iota(jnp.int32, (ROWS, PAD), 1)
    codes = jnp.where(lane == 0, (pos // 128)[:, None], jnp.where(lane == 1, (pos % 128)[:, None], 0))
    own = jnp.concatenate([pooled[0], codes.astype(BF)], axis=1)
    images = jnp.concatenate(gather_xy(own))

    raw = text_emb[0].astype(F32)
    text_inv = lax.rsqrt(jnp.sum(raw * raw, axis=-1, keepdims=True) + 1e-06)
    text_unit = raw * text_inv
    near = jnp.concatenate(gather_z(text_unit.astype(BF)))
    texts = jnp.concatenate([near, flip(near, "core", NC, 1)])

    z, xl, y, core = (lax.axis_index(a) for a in ("z", "xl", "y", "core"))
    columns = []
    for c in (core, 1 - core):
        for o in Z_OFFSETS:
            start = (((lax.rem(z + o + NZ, NZ) * NX + xl) * NY + y) * NC + c) * ROWS
            columns.append(start + jnp.arange(ROWS, dtype=jnp.int32))
    columns = jnp.concatenate(columns)[None]

    loss, mine, other, weight = tile(scalars, images, w_img, texts, columns)

    weight_grad = sum_weight(weight.reshape(NC, 4, NY, 6 * NZ, D_EMB)) / 64.0
    mine = mine + flip(other, "core", NC, 1).astype(F32)
    text_dir = sum_over_z([mine[i * ROWS : (i + 1) * ROWS] for i in range(NZ)])
    text_grad = (
        text_dir - text_unit * jnp.sum(text_unit * text_dir, axis=-1, keepdims=True)
    ) * text_inv
    row_loss = sum_losses(loss.reshape(NX * NY, ROWS)) / (NX * NY * NZ * NC * ROWS)
    return row_loss[None], weight_grad, text_grad[None]


def solution(mesh):
    names = ("z", "xl", "y", "core", "rep")
    fine = Mesh(mesh.devices.reshape(NZ, NX, NY, NC, NR), names)
    blk = names[:4]
    return jax.shard_map(
        shards,
        mesh=fine,
        in_specs=(P("rep", blk, None), P(), P("rep", blk, None), P("rep", blk), P(), P()),
        out_specs=(P("rep", blk), P(names, None), P("rep", blk, None)),
        check_vma=False,
    )
```

```python
import jax
import jax.numpy as jnp
import numpy as np
from jax import lax
from jax.experimental import pallas as pl
from jax.experimental.pallas import tpu as pltpu
from jax.sharding import Mesh
from jax.sharding import PartitionSpec as P

NZ, NX, NY, NC, NR = 8, 2, 4, 2, 2
ROWS = 128
HALF = ROWS // 2
D_IMG = 1536
D_EMB = 1024
PAD = 128
IMGS = NZ * ROWS
TEXTS = NX * NY * NC * ROWS
STEP = 256
CHUNK = 512
BF, F32 = jnp.bfloat16, jnp.float32
Z_OFFSETS = (0, -1, 1, -2, 2, -3, 3, 4)


def shift(x, axis, n, by):
    return lax.ppermute(x, axis, [(i, (i + by) % n) for i in range(n)])


def flip(x, axis, n, bit=1):
    return lax.ppermute(x, axis, [(i, i ^ bit) for i in range(n)])


def exchange(x, axes):
    return lax.all_to_all(x, axes, 0, 0)


def gather(image, text):
    down, up = [image], [image]
    for k in range(3):
        down.append(shift(down[-1], "z", NZ, 1))
        up.append(shift(up[-1], "z", NZ, -1))
        if k == 0:
            copies = jnp.broadcast_to(text, (NX * NY, *text.shape))
            down[1], up[1], copies = lax.optimization_barrier((down[1], up[1], copies))
            near = exchange(copies, ("xl", "y")).reshape(NX * NY * ROWS, D_EMB)
        if k == 1:
            down[2], up[2] = lax.optimization_barrier((down[2], up[2]))
    down[3], up[3], near = lax.optimization_barrier((down[3], up[3], near))
    far = [shift(down[3][:HALF], "z", NZ, 1), shift(up[3][HALF:], "z", NZ, -1)]
    images = [image, down[1], up[1], down[2], up[2], down[3], up[3]] + far
    return images, [near, flip(near, "core", NC)]


def halve(w, dim, here, axis, n, bit, kind):
    mine = lax.dynamic_index_in_dim(w, here, dim, keepdims=False)
    other = lax.dynamic_index_in_dim(w, 1 - here, dim, keepdims=False)
    return mine + flip(other.astype(kind), axis, n, bit).astype(F32)


def halve_both(w, dim, losses, here, bit):
    mine = lax.dynamic_index_in_dim(w, here, dim, keepdims=False)
    other = lax.dynamic_index_in_dim(w, 1 - here, dim, keepdims=False)
    mine_l = lax.dynamic_index_in_dim(losses, here, 0, keepdims=False)
    other_l = lax.dynamic_index_in_dim(losses, 1 - here, 0, keepdims=False).reshape(-1)
    high = lax.reduce_precision(other_l, 8, 7)
    pair = jnp.concatenate([high, other_l - high]).astype(BF)
    wide, n = w.shape[-1], pair.shape[0]
    tail = jnp.pad(pair, (0, 16 * wide - n)).reshape(16, wide)
    got = flip(jnp.concatenate([other.astype(BF).reshape(-1, wide), tail]), "z", NZ, bit)
    got_w = got[:-16].reshape(other.shape).astype(F32)
    got_l = got[-16:].reshape(-1)[:n].astype(F32).reshape(2, *mine_l.shape)
    return mine + got_w, mine_l + got_l[0] + got_l[1]


def sum_weight(w, losses, beside):
    z, xl, y, core, rep = (lax.axis_index(a) for a in ("z", "xl", "y", "core", "rep"))
    w = w.reshape(2, 2, 2, NX, 2, 2, 24, D_EMB // 2)
    losses = losses.reshape(2, 2, 2, ROWS).transpose(2, 1, 0, 3)
    half = D_EMB // 4
    z_bits = z // 4, lax.rem(z // 2, 2), lax.rem(z, 2)
    a, b = w[..., :half], w[..., half:]
    a, losses = halve_both(a, 2, losses, z_bits[2], 1)
    b = halve(b, 3, xl, "xl", NX, 1, BF)
    a = halve(a, 2, xl, "xl", NX, 1, BF)
    b = halve(b, 2, z_bits[2], "z", NZ, 1, BF)
    w = jnp.concatenate([a, b], axis=-1)
    w, beside = lax.optimization_barrier((w, beside))
    w, losses = halve_both(w, 1, losses, z_bits[1], 2)
    w, losses = halve_both(w, 0, losses, z_bits[0], 4)
    w = halve(w, 0, y // 2, "y", NY, 2, F32)
    w = halve(w, 0, lax.rem(y, 2), "y", NY, 1, F32)
    w = halve(w.reshape(NC, NR, 6, D_EMB // 2), 1, rep, "rep", NR, 1, F32)
    own = lax.dynamic_index_in_dim(w, core, 0, keepdims=False)
    got = flip(lax.dynamic_index_in_dim(w, 1 - core, 0, keepdims=False), "core", NC)
    w = jnp.where(core == 0, jnp.concatenate([own, got], 1), jnp.concatenate([got, own], 1))
    return w, losses, beside


def in_order(losses, z):
    at = {o: losses[i * ROWS : (i + 1) * ROWS] for i, o in enumerate(Z_OFFSETS)}
    ring = [at[o if o < 5 else o - NZ] for o in range(NZ)]
    return lax.dynamic_slice_in_dim(jnp.stack(ring + ring), NZ - z, NZ, 0)


NN = (((1,), (0,)), ((), ()))
NT = (((1,), (1,)), ((), ()))
TN = (((0,), (0,)), ((), ()))


def dot(a, b, dims, precision=None):
    return lax.dot_general(a, b, dims, precision=precision, preferred_element_type=F32)


def reciprocal(x):
    return pltpu.reciprocal(x, approx=True)


def pair_terms(products, hit, scale, shift_value):
    signed = jnp.where(hit, -scale, scale)
    e = jnp.exp(products * signed + jnp.where(hit, -shift_value, shift_value))
    u = 1.0 + e
    coeffs = (e * reciprocal(u) * signed).astype(BF)
    w = e.shape[1] // 4
    e4 = [e[:, k * w : (k + 1) * w] for k in range(4)]
    p = e4[0] + e4[1] * u[:, :w]
    q = e4[2] + e4[3] * u[:, 2 * w : 3 * w]
    g = p + q * (1.0 + p)
    v = 1.0 + g
    losses = jnp.log(v) + (g - (v - 1.0)) * reciprocal(v)
    return coeffs, losses


def fold(x):
    total = x[:, :128]
    for k in range(1, x.shape[1] // 128):
        total = total + x[:, k * 128 : (k + 1) * 128]
    return total


def tile_kernel(scalars, numbers, *refs):
    images, (w_img, *texts) = refs[:9], refs[9:12]
    loss, t_mine, t_other, w_mine, w_other, image, back, low_all, coeffs = refs[12:]
    step = pl.program_id(0)
    scale, shift_value = scalars[0], scalars[1]

    @pl.when(step == 0)
    def _():
        at = 0
        for b in images:
            image[at : at + b.shape[0], :] = b[...]
            at += b.shape[0]

    rows = pl.ds(pl.multiple_of(step * STEP, STEP), STEP)
    codes = image[rows, D_IMG:].astype(F32)
    positive = (codes[:, 0:1] * 128.0 + codes[:, 1:2]).astype(jnp.int32)
    projected = dot(image[rows, :D_IMG], w_img[...], NN)
    inverse = lax.rsqrt(jnp.sum(projected * projected, axis=1, keepdims=True) + 1e-06)
    unit = projected * inverse
    low = unit.astype(BF)
    low_all[rows, :] = low
    lane = lax.broadcasted_iota(jnp.int32, (1, ROWS), 1)
    chunks = [slice(k * CHUNK, (k + 1) * CHUNK) for k in range(TEXTS // CHUNK)]
    text = [t[k : k + CHUNK, :] for t in texts for k in range(0, t.shape[0], CHUNK)]
    products = dot(low, text[0], NT)
    direction = total = None
    for k, at in enumerate(chunks):
        here = products
        if k + 1 < len(chunks):
            products = dot(low, text[k + 1], NT)
        per = CHUNK // ROWS
        columns = jnp.concatenate([numbers[k * per + j] + lane for j in range(per)], axis=1)
        c, losses = pair_terms(here, positive == columns, scale, shift_value)
        coeffs[rows, at] = c
        d = dot(c, text[k], NN)
        direction = d if direction is None else direction + d
        total = fold(losses) if total is None else total + fold(losses)
    loss[...] = dot(jnp.ones((8, 128), F32), total, NT, lax.Precision.HIGHEST)
    dots = jnp.sum(unit * direction, axis=1, keepdims=True)
    back[rows, :] = ((direction - unit * dots) * inverse).astype(BF)

    @pl.when(step == pl.num_programs(0) - 1)
    def _():
        core = numbers[NX * NY * NC]
        half = D_EMB // 2
        for ref, c in ((w_other, 1 - core), (w_mine, core)):
            right = back[:, pl.ds(pl.multiple_of(c * half, half), half)]
            for k in range(0, D_IMG, 512):
                ref[k : k + 512, :] = dot(image[:, k : k + 512], right, TN).astype(ref.dtype)
        for part, ref in ((1, t_other), (0, t_mine)):
            for k in range(0, TEXTS // 2, 512):
                left = coeffs[:, part * (TEXTS // 2) + k : part * (TEXTS // 2) + k + 512]
                ref[k : k + 512, :] = dot(left, low_all[...], TN).astype(ref.dtype)


def tile(scalars, numbers, images, w_img, texts):
    def whole(x):
        return pl.BlockSpec(x.shape, lambda i: (0,) * len(x.shape), pipeline_mode=pl.Buffered(1))

    smem = pl.BlockSpec(memory_space=pltpu.SMEM)
    out_shape = [
        jax.ShapeDtypeStruct((8, IMGS), F32),
        jax.ShapeDtypeStruct((TEXTS // 2, D_EMB), BF),
        jax.ShapeDtypeStruct((TEXTS // 2, D_EMB), BF),
        jax.ShapeDtypeStruct((D_IMG, D_EMB // 2), F32),
        jax.ShapeDtypeStruct((D_IMG, D_EMB // 2), BF),
    ]
    arrays = [*images, w_img, *texts]
    return pl.pallas_call(
        tile_kernel,
        grid=(IMGS // STEP,),
        in_specs=[smem, smem] + [whole(a) for a in arrays],
        out_specs=[
            pl.BlockSpec((8, STEP), lambda i: (0, i)),
            whole(out_shape[1]),
            whole(out_shape[2]),
            whole(out_shape[3]),
            whole(out_shape[4]),
        ],
        out_shape=out_shape,
        scratch_shapes=[
            pltpu.VMEM((IMGS, D_IMG + PAD), BF),
            pltpu.VMEM((IMGS, D_EMB), BF),
            pltpu.VMEM((IMGS, D_EMB), BF),
            pltpu.VMEM((IMGS, TEXTS), BF),
        ],
        compiler_params=pltpu.CompilerParams(vmem_limit_bytes=56 * 2**20),
        cost_estimate=pl.CostEstimate(
            flops=2 * IMGS * D_EMB * (3 * TEXTS + 2 * D_IMG),
            bytes_accessed=24 * 2**20,
            transcendentals=3 * IMGS * TEXTS,
        ),
    )(scalars, numbers, *arrays)


def shards(pooled, w_img, text_emb, pos_index, log_scale, bias):
    z, xl, y, core = (lax.axis_index(a) for a in ("z", "xl", "y", "core"))
    scalars = jnp.stack([jnp.exp(log_scale[0]), bias[0]])
    pos = pos_index[0]
    lane = lax.broadcasted_iota(jnp.int32, (ROWS, PAD), 1)
    codes = jnp.where(lane == 0, (pos // 128)[:, None], jnp.where(lane == 1, (pos % 128)[:, None], 0))
    own = jnp.concatenate([pooled[0], codes.astype(BF)], axis=1)

    raw = text_emb[0].astype(F32)
    text_inv = lax.rsqrt(jnp.sum(raw * raw, axis=-1, keepdims=True) + 1e-06)
    text_unit = raw * text_inv
    images, texts = gather(own, text_unit.astype(BF))

    plane = np.arange(NX * NY, dtype=np.int32)
    starts = lambda c: ((z * NX * NY + plane) * NC + c) * ROWS
    numbers = jnp.concatenate([starts(core), starts(1 - core), core[None]]).astype(jnp.int32)

    loss, t_mine, t_other, w_mine, w_other = tile(scalars, numbers, images, w_img, texts)
    t_sum = t_mine.astype(F32) + flip(t_other, "core", NC).astype(F32)
    w = w_mine + flip(w_other, "core", NC).astype(F32)
    blocks = exchange(t_sum.astype(BF).reshape(NX * NY, ROWS, D_EMB), ("xl", "y"))
    weight_sum, losses, blocks = sum_weight(w, in_order(loss[0], z), blocks)
    text_dir = jnp.sum(blocks.astype(F32), axis=0)
    weight_grad = weight_sum / 64.0
    text_grad = (
        text_dir - text_unit * jnp.sum(text_unit * text_dir, axis=-1, keepdims=True)
    ) * text_inv
    row_loss = losses / (NX * NY * NZ * NC * ROWS)
    return row_loss[None], weight_grad, text_grad[None]


def solution(mesh):
    names = ("z", "xl", "y", "core", "rep")
    fine = Mesh(mesh.devices.reshape(NZ, NX, NY, NC, NR), names)
    blk = names[:4]
    return jax.shard_map(
        shards,
        mesh=fine,
        in_specs=(P("rep", blk, None), P(), P("rep", blk, None), P("rep", blk), P(), P()),
        out_specs=(P("rep", blk), P(names, None), P("rep", blk, None)),
        check_vma=False,
    )
```

```python
import functools

import jax
import jax.numpy as jnp
import numpy as np
from jax import lax
from jax.experimental import pallas as pl
from jax.experimental.pallas import tpu as pltpu
from jax.sharding import Mesh
from jax.sharding import PartitionSpec as P

NZ, NX, NY, NC, NR = 8, 2, 4, 2, 2
ROWS = 128
HALF = ROWS // 2
D_IMG = 1536
D_EMB = 1024
PAD = 128
IMGS = NZ * ROWS
TEXTS = NX * NY * NC * ROWS
STEP = 256
CHUNK = 512
BF, F32 = jnp.bfloat16, jnp.float32
Z_OFFSETS = (0, -1, 1, -2, 2, -3, 3, 4)


def shift(x, axis, n, by):
    return lax.ppermute(x, axis, [(i, (i + by) % n) for i in range(n)])


def flip(x, axis, n, bit=1):
    return lax.ppermute(x, axis, [(i, i ^ bit) for i in range(n)])


def exchange(x, axes):
    return lax.all_to_all(x, axes, 0, 0)


def gather(image, text):
    down, up = [image], [image]
    for k in range(3):
        down.append(shift(down[-1], "z", NZ, 1))
        up.append(shift(up[-1], "z", NZ, -1))
        if k == 0:
            copies = jnp.broadcast_to(text, (NX * NY, *text.shape))
            down[1], up[1], copies = lax.optimization_barrier((down[1], up[1], copies))
            near = exchange(copies, ("xl", "y")).reshape(NX * NY * ROWS, D_EMB)
        if k == 1:
            down[2], up[2] = lax.optimization_barrier((down[2], up[2]))
    down[3], up[3], near = lax.optimization_barrier((down[3], up[3], near))
    far = [shift(down[3][:HALF], "z", NZ, 1), shift(up[3][HALF:], "z", NZ, -1)]
    images = [image, down[1], up[1], down[2], up[2], down[3], up[3]] + far
    return images, [near, flip(near, "core", NC)]


def halve(w, dim, here, axis, n, bit, kind):
    mine = lax.dynamic_index_in_dim(w, here, dim, keepdims=False)
    other = lax.dynamic_index_in_dim(w, 1 - here, dim, keepdims=False)
    return mine + flip(other.astype(kind), axis, n, bit).astype(F32)


def halve_both(w, dim, losses, here, bit, kind):
    mine = lax.dynamic_index_in_dim(w, here, dim, keepdims=False)
    other = lax.dynamic_index_in_dim(w, 1 - here, dim, keepdims=False)
    mine_l = lax.dynamic_index_in_dim(losses, here, 0, keepdims=False)
    other_l = lax.dynamic_index_in_dim(losses, 1 - here, 0, keepdims=False).reshape(-1)
    if kind == BF:
        high = lax.reduce_precision(other_l, 8, 7)
        other_l = jnp.concatenate([high, other_l - high]).astype(BF)
    wide, n = w.shape[-1], other_l.shape[0]
    tail = jnp.pad(other_l, (0, 16 * wide - n)).reshape(16, wide)
    got = flip(jnp.concatenate([other.astype(kind).reshape(-1, wide), tail]), "z", NZ, bit)
    got_w = got[:-16].reshape(other.shape).astype(F32)
    got_l = got[-16:].reshape(-1)[:n].astype(F32).reshape(-1, *mine_l.shape)
    return mine + got_w, mine_l + jnp.sum(got_l, axis=0)


def sum_weight(w, losses, blocks):
    z, xl, y, core, rep = (lax.axis_index(a) for a in ("z", "xl", "y", "core", "rep"))
    w = w.reshape(2, 2, 2, NX, 2, 2, 24, D_EMB // 2)
    losses = losses.reshape(2, 2, 2, ROWS).transpose(2, 1, 0, 3)
    half = D_EMB // 4
    z_bits = z // 4, lax.rem(z // 2, 2), lax.rem(z, 2)
    a, b = w[..., :half], w[..., half:]
    a, losses = halve_both(a, 2, losses, z_bits[2], 1, BF)
    b = halve(b, 4, y // 2, "y", NY, 2, BF)
    a = halve(a, 3, y // 2, "y", NY, 2, BF)
    b = halve(b, 2, z_bits[2], "z", NZ, 1, BF)
    w = jnp.concatenate([a, b], axis=-1)
    blocks = exchange(blocks, ("xl", "y"))
    w = halve(w, 3, lax.rem(y, 2), "y", NY, 1, BF)
    w = halve(w, 2, xl, "xl", NX, 1, BF)
    w = halve(w.reshape(2, 2, NC, NR, 6, D_EMB // 2), 3, rep, "rep", NR, 1, F32)
    w, losses = halve_both(w, 1, losses, z_bits[1], 2, F32)
    w, losses = halve_both(w, 0, losses, z_bits[0], 4, F32)
    w, blocks = lax.optimization_barrier((w, blocks))
    own = lax.dynamic_index_in_dim(w, core, 0, keepdims=False)
    got = flip(lax.dynamic_index_in_dim(w, 1 - core, 0, keepdims=False), "core", NC)
    w = jnp.where(core == 0, jnp.concatenate([own, got], 1), jnp.concatenate([got, own], 1))
    return w, losses, blocks


def in_order(losses, z):
    at = {o: losses[i * ROWS : (i + 1) * ROWS] for i, o in enumerate(Z_OFFSETS)}
    ring = [at[o if o < 5 else o - NZ] for o in range(NZ)]
    return lax.dynamic_slice_in_dim(jnp.stack(ring + ring), NZ - z, NZ, 0)


NN = (((1,), (0,)), ((), ()))
NT = (((1,), (1,)), ((), ()))
TN = (((0,), (0,)), ((), ()))


def dot(a, b, dims, precision=None):
    return lax.dot_general(a, b, dims, precision=precision, preferred_element_type=F32)


def reciprocal(x):
    return pltpu.reciprocal(x, approx=True)


def pair_terms(products, hit, scale, shift_value):
    signed = jnp.where(hit, -scale, scale)
    e = jnp.exp(products * signed + jnp.where(hit, -shift_value, shift_value))
    u = 1.0 + e
    coeffs = (e * reciprocal(u) * signed).astype(BF)
    w = e.shape[1] // 4
    e4 = [e[:, k * w : (k + 1) * w] for k in range(4)]
    p = e4[0] + e4[1] * u[:, :w]
    q = e4[2] + e4[3] * u[:, 2 * w : 3 * w]
    g = p + q * (1.0 + p)
    v = 1.0 + g
    losses = jnp.log(v) + (g - (v - 1.0)) * reciprocal(v)
    return coeffs, losses


def fold(x):
    total = x[:, :128]
    for k in range(1, x.shape[1] // 128):
        total = total + x[:, k * 128 : (k + 1) * 128]
    return total


def tile_kernel(n_images, weigh, scalars, numbers, *refs):
    images, (w_img, *texts) = refs[:n_images], refs[n_images : n_images + 3]
    refs = refs[n_images + 3 :]
    if weigh:
        early, (early_back, loss, coeffs, low_out, w_mine, w_other, image, back) = refs[:4], refs[4:]
    else:
        loss, coeffs, low_out, back_out, image = refs
    step = pl.program_id(0)
    scale, shift_value = scalars[0], scalars[1]

    @pl.when(step == 0)
    def _():
        at = 0
        for b in images:
            image[at : at + b.shape[0], :] = b[...]
            at += b.shape[0]

    rows = pl.ds(pl.multiple_of(step * STEP, STEP), STEP)
    codes = image[rows, D_IMG:].astype(F32)
    positive = (codes[:, 0:1] * 128.0 + codes[:, 1:2]).astype(jnp.int32)
    projected = dot(image[rows, :D_IMG], w_img[...], NN)
    inverse = lax.rsqrt(jnp.sum(projected * projected, axis=1, keepdims=True) + 1e-06)
    unit = projected * inverse
    low = unit.astype(BF)
    low_out[...] = low
    lane = lax.broadcasted_iota(jnp.int32, (1, ROWS), 1)
    chunks = [slice(k * CHUNK, (k + 1) * CHUNK) for k in range(TEXTS // CHUNK)]
    text = [t[k : k + CHUNK, :] for t in texts for k in range(0, t.shape[0], CHUNK)]
    products = dot(low, text[0], NT)
    direction = total = None
    for k, at in enumerate(chunks):
        here = products
        if k + 1 < len(chunks):
            products = dot(low, text[k + 1], NT)
        per = CHUNK // ROWS
        columns = jnp.concatenate([numbers[k * per + j] + lane for j in range(per)], axis=1)
        c, losses = pair_terms(here, positive == columns, scale, shift_value)
        coeffs[:, at] = c
        d = dot(c, text[k], NN)
        direction = d if direction is None else direction + d
        total = fold(losses) if total is None else total + fold(losses)
    loss[...] = dot(jnp.ones((8, 128), F32), total, NT, lax.Precision.HIGHEST)
    dots = jnp.sum(unit * direction, axis=1, keepdims=True)
    result = ((direction - unit * dots) * inverse).astype(BF)
    if not weigh:
        back_out[...] = result
        return
    back[rows, :] = result

    @pl.when(step == pl.num_programs(0) - 1)
    def _():
        core = numbers[NX * NY * NC]
        half = D_EMB // 2
        for ref, c in ((w_other, 1 - core), (w_mine, core)):
            columns = pl.ds(pl.multiple_of(c * half, half), half)
            right, early_right = back[:, columns], early_back[:, columns]
            for k in range(0, D_IMG, 512):
                left = jnp.concatenate([e[:, k : k + 512] for e in early])
                w = dot(image[:, k : k + 512], right, TN) + dot(left, early_right, TN)
                ref[k : k + 512, :] = w.astype(ref.dtype)


def tile(scalars, numbers, images, w_img, texts, early=None):
    def whole(x):
        return pl.BlockSpec(x.shape, lambda i: (0,) * len(x.shape), pipeline_mode=pl.Buffered(1))

    rows = lambda n: pl.BlockSpec((STEP, n), lambda i: (i, 0))
    smem = pl.BlockSpec(memory_space=pltpu.SMEM)
    half = IMGS // 2
    out_shape = [
        jax.ShapeDtypeStruct((8, half), F32),
        jax.ShapeDtypeStruct((half, TEXTS), BF),
        jax.ShapeDtypeStruct((half, D_EMB), BF),
    ]
    out_specs = [pl.BlockSpec((8, STEP), lambda i: (0, i)), rows(TEXTS), rows(D_EMB)]
    scratch = [pltpu.VMEM((half, D_IMG + PAD), BF)]
    arrays = [*images, w_img, *texts]
    flops = 2 * half * D_EMB * (2 * TEXTS + D_IMG)
    if early is None:
        out_shape += [jax.ShapeDtypeStruct((half, D_EMB), BF)]
        out_specs += [rows(D_EMB)]
    else:
        arrays += [*early[0], early[1]]
        out_shape += [
            jax.ShapeDtypeStruct((D_IMG, D_EMB // 2), F32),
            jax.ShapeDtypeStruct((D_IMG, D_EMB // 2), BF),
        ]
        out_specs += [whole(out_shape[3]), whole(out_shape[4])]
        scratch += [pltpu.VMEM((half, D_EMB), BF)]
        flops += 2 * IMGS * D_EMB * D_IMG
    return pl.pallas_call(
        functools.partial(tile_kernel, len(images), early is not None),
        grid=(half // STEP,),
        in_specs=[smem, smem] + [whole(a) for a in arrays],
        out_specs=out_specs,
        out_shape=out_shape,
        scratch_shapes=scratch,
        compiler_params=pltpu.CompilerParams(vmem_limit_bytes=56 * 2**20),
        cost_estimate=pl.CostEstimate(
            flops=flops, bytes_accessed=16 * 2**20, transcendentals=2 * half * TEXTS
        ),
    )(scalars, numbers, *arrays)


def text_kernel(coeffs_a, coeffs_b, low_a, low_b, mine, other):
    total = dot(coeffs_a[...], low_a[...], TN) + dot(coeffs_b[...], low_b[...], TN)
    step, half = pl.program_id(0), pl.num_programs(0) // 2

    @pl.when(step < half)
    def _():
        other[...] = total.astype(BF)

    @pl.when(step >= half)
    def _():
        mine[...] = total.astype(BF)


def text_directions(coeffs, low):
    block = 512
    half = IMGS // 2
    steps = TEXTS // block // 2
    column = pl.BlockSpec((half, block), lambda i: (0, (i + steps) % (2 * steps)))
    keep = pl.BlockSpec((half, D_EMB), lambda i: (0, 0), pipeline_mode=pl.Buffered(1))
    return pl.pallas_call(
        text_kernel,
        grid=(TEXTS // block,),
        in_specs=[column, column, keep, keep],
        out_specs=[
            pl.BlockSpec((block, D_EMB), lambda i: (jnp.maximum(i - steps, 0), 0)),
            pl.BlockSpec((block, D_EMB), lambda i: (jnp.minimum(i, steps - 1), 0)),
        ],
        out_shape=[jax.ShapeDtypeStruct((TEXTS // 2, D_EMB), BF)] * 2,
        compiler_params=pltpu.CompilerParams(vmem_limit_bytes=60 * 2**20),
        cost_estimate=pl.CostEstimate(
            flops=2 * IMGS * D_EMB * TEXTS, bytes_accessed=10 * 2**20, transcendentals=0
        ),
    )(*coeffs, *low)


def shards(pooled, w_img, text_emb, pos_index, log_scale, bias):
    z, xl, y, core = (lax.axis_index(a) for a in ("z", "xl", "y", "core"))
    scalars = jnp.stack([jnp.exp(log_scale[0]), bias[0]])
    pos = pos_index[0]
    lane = lax.broadcasted_iota(jnp.int32, (ROWS, PAD), 1)
    codes = jnp.where(lane == 0, (pos // 128)[:, None], jnp.where(lane == 1, (pos % 128)[:, None], 0))
    own = jnp.concatenate([pooled[0], codes.astype(BF)], axis=1)

    raw = text_emb[0].astype(F32)
    text_inv = lax.rsqrt(jnp.sum(raw * raw, axis=-1, keepdims=True) + 1e-06)
    text_unit = raw * text_inv
    images, texts = gather(own, text_unit.astype(BF))

    plane = np.arange(NX * NY, dtype=np.int32)
    starts = lambda c: ((z * NX * NY + plane) * NC + c) * ROWS
    numbers = jnp.concatenate([starts(core), starts(1 - core), core[None]]).astype(jnp.int32)

    early_loss, early_coeffs, early_low, early_back = tile(scalars, numbers, images[:4], w_img, texts)
    late = tile(scalars, numbers, images[4:], w_img, texts, (images[:4], early_back))
    late_loss, late_coeffs, late_low, w_mine, w_other = late
    loss = jnp.concatenate([early_loss[0], late_loss[0]])
    w = w_mine + flip(w_other, "core", NC).astype(F32)
    late_coeffs, w = lax.optimization_barrier((late_coeffs, w))
    t_mine, t_other = text_directions((early_coeffs, late_coeffs), (early_low, late_low))
    t_sum = t_mine.astype(F32) + flip(t_other, "core", NC).astype(F32)
    blocks = t_sum.astype(BF).reshape(NX * NY, ROWS, D_EMB)
    weight_sum, losses, blocks = sum_weight(w, in_order(loss, z), blocks)
    text_dir = jnp.sum(blocks.astype(F32), axis=0)
    weight_grad = weight_sum / 64.0
    text_grad = (
        text_dir - text_unit * jnp.sum(text_unit * text_dir, axis=-1, keepdims=True)
    ) * text_inv
    row_loss = losses / (NX * NY * NZ * NC * ROWS)
    return row_loss[None], weight_grad, text_grad[None]


def solution(mesh):
    names = ("z", "xl", "y", "core", "rep")
    fine = Mesh(mesh.devices.reshape(NZ, NX, NY, NC, NR), names)
    blk = names[:4]
    return jax.shard_map(
        shards,
        mesh=fine,
        in_specs=(P("rep", blk, None), P(), P("rep", blk, None), P("rep", blk), P(), P()),
        out_specs=(P("rep", blk), P(names, None), P("rep", blk, None)),
        check_vma=False,
    )
```

```python
import functools

import jax
import jax.numpy as jnp
import numpy as np
from jax import lax
from jax.experimental import pallas as pl
from jax.experimental.pallas import tpu as pltpu
from jax.sharding import Mesh
from jax.sharding import PartitionSpec as P

NZ, NX, NY, NC, NR = 8, 2, 4, 2, 2
ROWS = 128
HALF = ROWS // 2
D_IMG = 1536
D_EMB = 1024
PAD = 128
IMGS = NZ * ROWS
TEXTS = NX * NY * NC * ROWS
STEP = 256
CHUNK = 512
BF, F32 = jnp.bfloat16, jnp.float32
Z_OFFSETS = (0, -1, 1, -2, 2, -3, 3, 4)


def shift(x, axis, n, by):
    return lax.ppermute(x, axis, [(i, (i + by) % n) for i in range(n)])


def flip(x, axis, n, bit=1):
    return lax.ppermute(x, axis, [(i, i ^ bit) for i in range(n)])


def exchange(x, axes):
    return lax.all_to_all(x, axes, 0, 0)


def gather(image, text):
    copies = jnp.broadcast_to(text, (NX * NY, *text.shape))
    near = exchange(copies, ("xl", "y")).reshape(NX * NY * ROWS, D_EMB)
    down, up = [image], [image]
    for k in range(3):
        down.append(shift(down[-1], "z", NZ, 1))
        up.append(shift(up[-1], "z", NZ, -1))
        if k == 1:
            down[-1], up[-1], near = lax.optimization_barrier((down[-1], up[-1], near))
        elif k == 0:
            down[-1], up[-1] = lax.optimization_barrier((down[-1], up[-1]))
    images = [image, down[1], up[1], down[2], up[2], down[3], up[3]]
    return images, [near, flip(near, "core", NC)]


def gather_last(below, above):
    return [shift(below[:HALF], "z", NZ, 1), shift(above[HALF:], "z", NZ, -1)]


def halve(w, dim, here, axis, n, bit, kind):
    mine = lax.dynamic_index_in_dim(w, here, dim, keepdims=False)
    other = lax.dynamic_index_in_dim(w, 1 - here, dim, keepdims=False)
    return mine + flip(other.astype(kind), axis, n, bit).astype(F32)


def halve_both(w, dim, losses, here, bit, kind):
    mine = lax.dynamic_index_in_dim(w, here, dim, keepdims=False)
    other = lax.dynamic_index_in_dim(w, 1 - here, dim, keepdims=False)
    mine_l = lax.dynamic_index_in_dim(losses, here, 0, keepdims=False)
    other_l = lax.dynamic_index_in_dim(losses, 1 - here, 0, keepdims=False).reshape(-1)
    if kind == BF:
        high = lax.reduce_precision(other_l, 8, 7)
        other_l = jnp.concatenate([high, other_l - high]).astype(BF)
    wide, n = w.shape[-1], other_l.shape[0]
    tail = jnp.pad(other_l, (0, 16 * wide - n)).reshape(16, wide)
    got = flip(jnp.concatenate([other.astype(kind).reshape(-1, wide), tail]), "z", NZ, bit)
    got_w = got[:-16].reshape(other.shape).astype(F32)
    got_l = got[-16:].reshape(-1)[:n].astype(F32).reshape(-1, *mine_l.shape)
    return mine + got_w, mine_l + jnp.sum(got_l, axis=0)


def sum_weight(w, losses, blocks):
    z, xl, y, core, rep = (lax.axis_index(a) for a in ("z", "xl", "y", "core", "rep"))
    w = w.reshape(2, 2, 2, NX, 2, 2, 24, D_EMB // 2)
    losses = losses.reshape(2, 2, 2, ROWS).transpose(2, 1, 0, 3)
    half = D_EMB // 4
    z_bits = z // 4, lax.rem(z // 2, 2), lax.rem(z, 2)
    a, b = w[..., :half], w[..., half:]
    a, losses = halve_both(a, 2, losses, z_bits[2], 1, BF)
    b = halve(b, 4, y // 2, "y", NY, 2, BF)
    a = halve(a, 3, y // 2, "y", NY, 2, BF)
    b = halve(b, 2, z_bits[2], "z", NZ, 1, BF)
    w = jnp.concatenate([a, b], axis=-1)
    blocks = exchange(blocks, ("xl", "y"))
    w = halve(w, 3, lax.rem(y, 2), "y", NY, 1, BF)
    w = halve(w, 2, xl, "xl", NX, 1, BF)
    w = halve(w.reshape(2, 2, NC, NR, 6, D_EMB // 2), 3, rep, "rep", NR, 1, F32)
    w, losses = halve_both(w, 1, losses, z_bits[1], 2, F32)
    w, losses = halve_both(w, 0, losses, z_bits[0], 4, F32)
    w, blocks = lax.optimization_barrier((w, blocks))
    own = lax.dynamic_index_in_dim(w, core, 0, keepdims=False)
    got = flip(lax.dynamic_index_in_dim(w, 1 - core, 0, keepdims=False), "core", NC)
    w = jnp.where(core == 0, jnp.concatenate([own, got], 1), jnp.concatenate([got, own], 1))
    return w, losses, blocks


def in_order(losses, z):
    at = {o: losses[i * ROWS : (i + 1) * ROWS] for i, o in enumerate(Z_OFFSETS)}
    ring = [at[o if o < 5 else o - NZ] for o in range(NZ)]
    return lax.dynamic_slice_in_dim(jnp.stack(ring + ring), NZ - z, NZ, 0)


NN = (((1,), (0,)), ((), ()))
NT = (((1,), (1,)), ((), ()))
TN = (((0,), (0,)), ((), ()))


def dot(a, b, dims, precision=None):
    return lax.dot_general(a, b, dims, precision=precision, preferred_element_type=F32)


def reciprocal(x):
    return pltpu.reciprocal(x, approx=True)


def pair_terms(products, hit, scale, shift_value):
    signed = jnp.where(hit, -scale, scale)
    e = jnp.exp(products * signed + jnp.where(hit, -shift_value, shift_value))
    u = 1.0 + e
    coeffs = (e * reciprocal(u) * signed).astype(BF)
    w = e.shape[1] // 4
    e4 = [e[:, k * w : (k + 1) * w] for k in range(4)]
    p = e4[0] + e4[1] * u[:, :w]
    q = e4[2] + e4[3] * u[:, 2 * w : 3 * w]
    g = p + q * (1.0 + p)
    v = 1.0 + g
    losses = jnp.log(v) + (g - (v - 1.0)) * reciprocal(v)
    return coeffs, losses


def fold(x):
    total = x[:, :128]
    for k in range(1, x.shape[1] // 128):
        total = total + x[:, k * 128 : (k + 1) * 128]
    return total


def tile_kernel(n_images, n_early, scalars, numbers, *refs):
    weigh = n_early > 0
    images, (w_img, *texts) = refs[:n_images], refs[n_images : n_images + 3]
    refs = refs[n_images + 3 :]
    if weigh:
        early, early_back, refs = refs[:n_early], refs[n_early : n_early + 2], refs[n_early + 2 :]
        loss, coeffs, low_out, w_mine, w_other, image, back = refs
    else:
        loss, coeffs, low_out, back_out, image = refs
    step = pl.program_id(0)
    scale, shift_value = scalars[0], scalars[1]

    @pl.when(step == 0)
    def _():
        at = 0
        for b in images:
            image[at : at + b.shape[0], :] = b[...]
            at += b.shape[0]

    rows = pl.ds(pl.multiple_of(step * STEP, STEP), STEP)
    codes = image[rows, D_IMG:].astype(F32)
    positive = (codes[:, 0:1] * 128.0 + codes[:, 1:2]).astype(jnp.int32)
    projected = dot(image[rows, :D_IMG], w_img[...], NN)
    inverse = lax.rsqrt(jnp.sum(projected * projected, axis=1, keepdims=True) + 1e-06)
    unit = projected * inverse
    low = unit.astype(BF)
    low_out[...] = low
    lane = lax.broadcasted_iota(jnp.int32, (1, ROWS), 1)
    chunks = [slice(k * CHUNK, (k + 1) * CHUNK) for k in range(TEXTS // CHUNK)]
    text = [t[k : k + CHUNK, :] for t in texts for k in range(0, t.shape[0], CHUNK)]
    products = dot(low, text[0], NT)
    direction = total = None
    for k, at in enumerate(chunks):
        here = products
        if k + 1 < len(chunks):
            products = dot(low, text[k + 1], NT)
        per = CHUNK // ROWS
        columns = jnp.concatenate([numbers[k * per + j] + lane for j in range(per)], axis=1)
        c, losses = pair_terms(here, positive == columns, scale, shift_value)
        coeffs[:, at] = c
        d = dot(c, text[k], NN)
        direction = d if direction is None else direction + d
        total = fold(losses) if total is None else total + fold(losses)
    loss[...] = dot(jnp.ones((8, 128), F32), total, NT, lax.Precision.HIGHEST)
    dots = jnp.sum(unit * direction, axis=1, keepdims=True)
    result = ((direction - unit * dots) * inverse).astype(BF)
    if not weigh:
        back_out[...] = result
        return
    back[rows, :] = result

    @pl.when(step == pl.num_programs(0) - 1)
    def _():
        core = numbers[NX * NY * NC]
        half = D_EMB // 2
        for ref, c in ((w_other, 1 - core), (w_mine, core)):
            columns = pl.ds(pl.multiple_of(c * half, half), half)
            for k in range(0, D_IMG, 512):
                at = slice(k, k + 512)
                w = dot(image[:, at], back[:, columns], TN)
                done = 0
                for part in early_back:
                    n = part.shape[0] // ROWS
                    left = jnp.concatenate([e[:, at] for e in early[done : done + n]])
                    w = w + dot(left, part[:, columns], TN)
                    done += n
                ref[k : k + 512, :] = w.astype(ref.dtype)


def tile(scalars, numbers, images, w_img, texts, early=None):
    def whole(x):
        return pl.BlockSpec(x.shape, lambda i: (0,) * len(x.shape), pipeline_mode=pl.Buffered(1))

    rows = lambda n: pl.BlockSpec((STEP, n), lambda i: (i, 0))
    smem = pl.BlockSpec(memory_space=pltpu.SMEM)
    half = sum(b.shape[0] for b in images)
    out_shape = [
        jax.ShapeDtypeStruct((8, half), F32),
        jax.ShapeDtypeStruct((half, TEXTS), BF),
        jax.ShapeDtypeStruct((half, D_EMB), BF),
    ]
    out_specs = [pl.BlockSpec((8, STEP), lambda i: (0, i)), rows(TEXTS), rows(D_EMB)]
    scratch = [pltpu.VMEM((half, D_IMG + PAD), BF)]
    arrays = [*images, w_img, *texts]
    flops = 2 * half * D_EMB * (2 * TEXTS + D_IMG)
    if early is None:
        out_shape += [jax.ShapeDtypeStruct((half, D_EMB), BF)]
        out_specs += [rows(D_EMB)]
    else:
        arrays += [*early[0], *early[1]]
        out_shape += [
            jax.ShapeDtypeStruct((D_IMG, D_EMB // 2), F32),
            jax.ShapeDtypeStruct((D_IMG, D_EMB // 2), BF),
        ]
        out_specs += [whole(out_shape[3]), whole(out_shape[4])]
        scratch += [pltpu.VMEM((half, D_EMB), BF)]
        flops += 2 * IMGS * D_EMB * D_IMG
    return pl.pallas_call(
        functools.partial(tile_kernel, len(images), len(early[0]) if early else 0),
        grid=(half // STEP,),
        in_specs=[smem, smem] + [whole(a) for a in arrays],
        out_specs=out_specs,
        out_shape=out_shape,
        scratch_shapes=scratch,
        compiler_params=pltpu.CompilerParams(vmem_limit_bytes=56 * 2**20),
        cost_estimate=pl.CostEstimate(
            flops=flops, bytes_accessed=16 * 2**20, transcendentals=2 * half * TEXTS
        ),
    )(scalars, numbers, *arrays)


def text_kernel(*refs):
    coeffs, low, (mine, other) = refs[:3], refs[3:6], refs[6:]
    total = sum(dot(c[...], v[...], TN) for c, v in zip(coeffs, low))
    step, half = pl.program_id(0), pl.num_programs(0) // 2

    @pl.when(step < half)
    def _():
        other[...] = total.astype(BF)

    @pl.when(step >= half)
    def _():
        mine[...] = total.astype(BF)


def text_directions(coeffs, low):
    block = 512
    steps = TEXTS // block // 2
    column = lambda c: pl.BlockSpec((c.shape[0], block), lambda i: (0, (i + steps) % (2 * steps)))
    keep = lambda v: pl.BlockSpec(v.shape, lambda i: (0, 0), pipeline_mode=pl.Buffered(1))
    return pl.pallas_call(
        text_kernel,
        grid=(TEXTS // block,),
        in_specs=[*map(column, coeffs), *map(keep, low)],
        out_specs=[
            pl.BlockSpec((block, D_EMB), lambda i: (jnp.maximum(i - steps, 0), 0)),
            pl.BlockSpec((block, D_EMB), lambda i: (jnp.minimum(i, steps - 1), 0)),
        ],
        out_shape=[jax.ShapeDtypeStruct((TEXTS // 2, D_EMB), BF)] * 2,
        compiler_params=pltpu.CompilerParams(vmem_limit_bytes=60 * 2**20),
        cost_estimate=pl.CostEstimate(
            flops=2 * IMGS * D_EMB * TEXTS, bytes_accessed=10 * 2**20, transcendentals=0
        ),
    )(*coeffs, *low)


def shards(pooled, w_img, text_emb, pos_index, log_scale, bias):
    z, xl, y, core = (lax.axis_index(a) for a in ("z", "xl", "y", "core"))
    scalars = jnp.stack([jnp.exp(log_scale[0]), bias[0]])
    pos = pos_index[0]
    lane = lax.broadcasted_iota(jnp.int32, (ROWS, PAD), 1)
    codes = jnp.where(lane == 0, (pos // 128)[:, None], jnp.where(lane == 1, (pos % 128)[:, None], 0))
    own = jnp.concatenate([pooled[0], codes.astype(BF)], axis=1)

    raw = text_emb[0].astype(F32)
    text_inv = lax.rsqrt(jnp.sum(raw * raw, axis=-1, keepdims=True) + 1e-06)
    text_unit = raw * text_inv
    images, texts = gather(own, text_unit.astype(BF))

    plane = np.arange(NX * NY, dtype=np.int32)
    starts = lambda c: ((z * NX * NY + plane) * NC + c) * ROWS
    numbers = jnp.concatenate([starts(core), starts(1 - core), core[None]]).astype(jnp.int32)

    first, second = images[:4], images[4:6]
    loss_a, coeffs_a, low_a, back_a = tile(scalars, numbers, first, w_img, texts)
    below, above, back_a = lax.optimization_barrier((images[5], images[6], back_a))
    last = [images[6], *gather_last(below, above)]
    loss_b, coeffs_b, low_b, back_b = tile(scalars, numbers, second, w_img, texts)
    early = (first + second, (back_a, back_b))
    loss_c, coeffs_c, low_c, w_mine, w_other = tile(scalars, numbers, last, w_img, texts, early)
    loss = jnp.concatenate([loss_a[0], loss_b[0], loss_c[0]])
    w = w_mine + flip(w_other, "core", NC).astype(F32)
    coeffs_c, w = lax.optimization_barrier((coeffs_c, w))
    t_mine, t_other = text_directions((coeffs_a, coeffs_b, coeffs_c), (low_a, low_b, low_c))
    t_sum = t_mine.astype(F32) + flip(t_other, "core", NC).astype(F32)
    blocks = t_sum.astype(BF).reshape(NX * NY, ROWS, D_EMB)
    weight_sum, losses, blocks = sum_weight(w, in_order(loss, z), blocks)
    text_dir = jnp.sum(blocks.astype(F32), axis=0)
    weight_grad = weight_sum / 64.0
    text_grad = (
        text_dir - text_unit * jnp.sum(text_unit * text_dir, axis=-1, keepdims=True)
    ) * text_inv
    row_loss = losses / (NX * NY * NZ * NC * ROWS)
    return row_loss[None], weight_grad, text_grad[None]


def solution(mesh):
    names = ("z", "xl", "y", "core", "rep")
    fine = Mesh(mesh.devices.reshape(NZ, NX, NY, NC, NR), names)
    blk = names[:4]
    return jax.shard_map(
        shards,
        mesh=fine,
        in_specs=(P("rep", blk, None), P(), P("rep", blk, None), P("rep", blk), P(), P()),
        out_specs=(P("rep", blk), P(names, None), P("rep", blk, None)),
        check_vma=False,
    )
```

```python
import functools

import jax
import jax.numpy as jnp
import numpy as np
from jax import lax
from jax.experimental import pallas as pl
from jax.experimental.pallas import tpu as pltpu
from jax.sharding import Mesh
from jax.sharding import PartitionSpec as P

NZ, NX, NY, NC, NR = 8, 2, 4, 2, 2
ROWS = 128
HALF = ROWS // 2
D_IMG = 1536
D_EMB = 1024
PAD = 128
IMGS = NZ * ROWS
TEXTS = NX * NY * NC * ROWS
STEP = 256
CHUNK = 512
BF, F32 = jnp.bfloat16, jnp.float32
Z_OFFSETS = (0, -1, 1, -2, 2, -3, 3, 4)


def shift(x, axis, n, by):
    return lax.ppermute(x, axis, [(i, (i + by) % n) for i in range(n)])


def flip(x, axis, n, bit=1):
    return lax.ppermute(x, axis, [(i, i ^ bit) for i in range(n)])


def exchange(x, axes):
    return lax.all_to_all(x, axes, 0, 0)


def gather(image, text, scalars, numbers):
    copies = jnp.broadcast_to(text, (NX * NY, *text.shape))
    near = exchange(copies, ("xl", "y")).reshape(NX * NY * ROWS, D_EMB)
    down, up = [image], [image]
    for k in range(3):
        down.append(shift(down[-1], "z", NZ, 1))
        up.append(shift(up[-1], "z", NZ, -1))
        if k == 1:
            down[-1], up[-1], near = lax.optimization_barrier((down[-1], up[-1], near))
        elif k == 0:
            tied = lax.optimization_barrier((down[-1], up[-1], scalars, numbers))
            down[-1], up[-1], scalars, numbers = tied
    images = [image, down[1], up[1], down[2], up[2], down[3], up[3]]
    return images, [near, flip(near, "core", NC)], scalars, numbers


def gather_last(below, above):
    return [shift(below[:HALF], "z", NZ, 1), shift(above[HALF:], "z", NZ, -1)]


def halve(w, dim, here, axis, n, bit, kind):
    mine = lax.dynamic_index_in_dim(w, here, dim, keepdims=False)
    other = lax.dynamic_index_in_dim(w, 1 - here, dim, keepdims=False)
    return mine + flip(other.astype(kind), axis, n, bit).astype(F32)


def halve_both(w, dim, losses, here, bit, kind):
    mine = lax.dynamic_index_in_dim(w, here, dim, keepdims=False)
    other = lax.dynamic_index_in_dim(w, 1 - here, dim, keepdims=False)
    mine_l = lax.dynamic_index_in_dim(losses, here, 0, keepdims=False)
    other_l = lax.dynamic_index_in_dim(losses, 1 - here, 0, keepdims=False).reshape(-1)
    if kind == BF:
        high = lax.reduce_precision(other_l, 8, 7)
        other_l = jnp.concatenate([high, other_l - high]).astype(BF)
    wide, n = w.shape[-1], other_l.shape[0]
    tail = jnp.pad(other_l, (0, 16 * wide - n)).reshape(16, wide)
    got = flip(jnp.concatenate([other.astype(kind).reshape(-1, wide), tail]), "z", NZ, bit)
    got_w = got[:-16].reshape(other.shape).astype(F32)
    got_l = got[-16:].reshape(-1)[:n].astype(F32).reshape(-1, *mine_l.shape)
    return mine + got_w, mine_l + jnp.sum(got_l, axis=0)


def sum_weight(w, losses, blocks):
    z, xl, y, core, rep = (lax.axis_index(a) for a in ("z", "xl", "y", "core", "rep"))
    w = w.reshape(2, 2, 2, NX, 2, 2, 24, D_EMB // 2)
    losses = losses.reshape(2, 2, 2, ROWS).transpose(2, 1, 0, 3)
    half = D_EMB // 4
    z_bits = z // 4, lax.rem(z // 2, 2), lax.rem(z, 2)
    a, b = w[..., :half], w[..., half:]
    a = halve(a, 2, z_bits[2], "z", NZ, 1, BF)
    b = halve(b, 4, y // 2, "y", NY, 2, BF)
    a = halve(a, 3, y // 2, "y", NY, 2, BF)
    b, losses = halve_both(b, 2, losses, z_bits[2], 1, BF)
    w = jnp.concatenate([a, b], axis=-1)
    blocks = exchange(blocks, ("xl", "y"))
    w = halve(w, 3, lax.rem(y, 2), "y", NY, 1, BF)
    w = halve(w, 2, xl, "xl", NX, 1, BF)
    w = halve(w.reshape(2, 2, NC, NR, 6, D_EMB // 2), 3, rep, "rep", NR, 1, F32)
    w, losses = halve_both(w, 1, losses, z_bits[1], 2, F32)
    w, losses = halve_both(w, 0, losses, z_bits[0], 4, F32)
    w, blocks = lax.optimization_barrier((w, blocks))
    own = lax.dynamic_index_in_dim(w, core, 0, keepdims=False)
    got = flip(lax.dynamic_index_in_dim(w, 1 - core, 0, keepdims=False), "core", NC)
    w = jnp.where(core == 0, jnp.concatenate([own, got], 1), jnp.concatenate([got, own], 1))
    return w, losses, blocks


def in_order(losses, z):
    at = {o: losses[i * ROWS : (i + 1) * ROWS] for i, o in enumerate(Z_OFFSETS)}
    ring = [at[o if o < 5 else o - NZ] for o in range(NZ)]
    return lax.dynamic_slice_in_dim(jnp.stack(ring + ring), NZ - z, NZ, 0)


NN = (((1,), (0,)), ((), ()))
NT = (((1,), (1,)), ((), ()))
TN = (((0,), (0,)), ((), ()))


def dot(a, b, dims, precision=None):
    return lax.dot_general(a, b, dims, precision=precision, preferred_element_type=F32)


def reciprocal(x):
    return pltpu.reciprocal(x, approx=True)


def pair_terms(products, hit, scale, shift_value):
    signed = jnp.where(hit, -scale, scale)
    e = jnp.exp(products * signed + jnp.where(hit, -shift_value, shift_value))
    u = 1.0 + e
    coeffs = (e * reciprocal(u) * signed).astype(BF)
    w = e.shape[1] // 4
    e4 = [e[:, k * w : (k + 1) * w] for k in range(4)]
    p = e4[0] + e4[1] * u[:, :w]
    q = e4[2] + e4[3] * u[:, 2 * w : 3 * w]
    g = p + q * (1.0 + p)
    v = 1.0 + g
    losses = jnp.log(v) + (g - (v - 1.0)) * reciprocal(v)
    return coeffs, losses


def fold(x):
    total = x[:, :128]
    for k in range(1, x.shape[1] // 128):
        total = total + x[:, k * 128 : (k + 1) * 128]
    return total


def tile_kernel(n_images, n_early, scalars, numbers, *refs):
    weigh = n_early > 0
    images, (w_img, *texts) = refs[:n_images], refs[n_images : n_images + 3]
    refs = refs[n_images + 3 :]
    if weigh:
        early, early_back, refs = refs[:n_early], refs[n_early : n_early + 2], refs[n_early + 2 :]
        loss, coeffs, low_out, w_mine, w_other, image, back = refs
    else:
        loss, coeffs, low_out, back_out, image = refs
    step = pl.program_id(0)
    scale, shift_value = scalars[0], scalars[1]

    @pl.when(step == 0)
    def _():
        at = 0
        for b in images:
            image[at : at + b.shape[0], :] = b[...]
            at += b.shape[0]

    rows = pl.ds(pl.multiple_of(step * STEP, STEP), STEP)
    codes = image[rows, D_IMG:].astype(F32)
    positive = (codes[:, 0:1] * 128.0 + codes[:, 1:2]).astype(jnp.int32)
    projected = dot(image[rows, :D_IMG], w_img[...], NN)
    inverse = lax.rsqrt(jnp.sum(projected * projected, axis=1, keepdims=True) + 1e-06)
    unit = projected * inverse
    low = unit.astype(BF)
    low_out[...] = low
    lane = lax.broadcasted_iota(jnp.int32, (1, ROWS), 1)
    chunks = [slice(k * CHUNK, (k + 1) * CHUNK) for k in range(TEXTS // CHUNK)]
    text = [t[k : k + CHUNK, :] for t in texts for k in range(0, t.shape[0], CHUNK)]
    products = dot(low, text[0], NT)
    direction = total = None
    for k, at in enumerate(chunks):
        here = products
        if k + 1 < len(chunks):
            products = dot(low, text[k + 1], NT)
        per = CHUNK // ROWS
        columns = jnp.concatenate([numbers[k * per + j] + lane for j in range(per)], axis=1)
        c, losses = pair_terms(here, positive == columns, scale, shift_value)
        coeffs[:, at] = c
        d = dot(c, text[k], NN)
        direction = d if direction is None else direction + d
        total = fold(losses) if total is None else total + fold(losses)
    loss[...] = dot(jnp.ones((8, 128), F32), total, NT, lax.Precision.HIGHEST)
    dots = jnp.sum(unit * direction, axis=1, keepdims=True)
    result = ((direction - unit * dots) * inverse).astype(BF)
    if not weigh:
        back_out[...] = result
        return
    back[rows, :] = result

    @pl.when(step == pl.num_programs(0) - 1)
    def _():
        core = numbers[NX * NY * NC]
        half = D_EMB // 2
        for ref, c in ((w_other, 1 - core), (w_mine, core)):
            columns = pl.ds(pl.multiple_of(c * half, half), half)
            for k in range(0, D_IMG, 512):
                at = slice(k, k + 512)
                w = dot(image[:, at], back[:, columns], TN)
                done = 0
                for part in early_back:
                    n = part.shape[0] // ROWS
                    left = jnp.concatenate([e[:, at] for e in early[done : done + n]])
                    w = w + dot(left, part[:, columns], TN)
                    done += n
                ref[k : k + 512, :] = w.astype(ref.dtype)


def tile(scalars, numbers, images, w_img, texts, early=None):
    def whole(x):
        return pl.BlockSpec(x.shape, lambda i: (0,) * len(x.shape), pipeline_mode=pl.Buffered(1))

    rows = lambda n: pl.BlockSpec((STEP, n), lambda i: (i, 0))
    smem = pl.BlockSpec(memory_space=pltpu.SMEM)
    half = sum(b.shape[0] for b in images)
    out_shape = [
        jax.ShapeDtypeStruct((8, half), F32),
        jax.ShapeDtypeStruct((half, TEXTS), BF),
        jax.ShapeDtypeStruct((half, D_EMB), BF),
    ]
    out_specs = [pl.BlockSpec((8, STEP), lambda i: (0, i)), rows(TEXTS), rows(D_EMB)]
    scratch = [pltpu.VMEM((half, D_IMG + PAD), BF)]
    arrays = [*images, w_img, *texts]
    flops = 2 * half * D_EMB * (2 * TEXTS + D_IMG)
    if early is None:
        out_shape += [jax.ShapeDtypeStruct((half, D_EMB), BF)]
        out_specs += [rows(D_EMB)]
    else:
        arrays += [*early[0], *early[1]]
        out_shape += [
            jax.ShapeDtypeStruct((D_IMG, D_EMB // 2), F32),
            jax.ShapeDtypeStruct((D_IMG, D_EMB // 2), BF),
        ]
        out_specs += [whole(out_shape[3]), whole(out_shape[4])]
        scratch += [pltpu.VMEM((half, D_EMB), BF)]
        flops += 2 * IMGS * D_EMB * D_IMG
    return pl.pallas_call(
        functools.partial(tile_kernel, len(images), len(early[0]) if early else 0),
        grid=(half // STEP,),
        in_specs=[smem, smem] + [whole(a) for a in arrays],
        out_specs=out_specs,
        out_shape=out_shape,
        scratch_shapes=scratch,
        compiler_params=pltpu.CompilerParams(vmem_limit_bytes=56 * 2**20),
        cost_estimate=pl.CostEstimate(
            flops=flops, bytes_accessed=16 * 2**20, transcendentals=2 * half * TEXTS
        ),
    )(scalars, numbers, *arrays)


def text_kernel(*refs):
    coeffs, low, (mine, other) = refs[:3], refs[3:6], refs[6:]
    total = sum(dot(c[...], v[...], TN) for c, v in zip(coeffs, low))
    step, half = pl.program_id(0), pl.num_programs(0) // 2

    @pl.when(step < half)
    def _():
        other[...] = total.astype(BF)

    @pl.when(step >= half)
    def _():
        mine[...] = total.astype(BF)


def text_directions(coeffs, low):
    block = 512
    steps = TEXTS // block // 2
    column = lambda c: pl.BlockSpec((c.shape[0], block), lambda i: (0, (i + steps) % (2 * steps)))
    keep = lambda v: pl.BlockSpec(v.shape, lambda i: (0, 0), pipeline_mode=pl.Buffered(1))
    return pl.pallas_call(
        text_kernel,
        grid=(TEXTS // block,),
        in_specs=[*map(column, coeffs), *map(keep, low)],
        out_specs=[
            pl.BlockSpec((block, D_EMB), lambda i: (jnp.maximum(i - steps, 0), 0)),
            pl.BlockSpec((block, D_EMB), lambda i: (jnp.minimum(i, steps - 1), 0)),
        ],
        out_shape=[jax.ShapeDtypeStruct((TEXTS // 2, D_EMB), BF)] * 2,
        compiler_params=pltpu.CompilerParams(vmem_limit_bytes=60 * 2**20),
        cost_estimate=pl.CostEstimate(
            flops=2 * IMGS * D_EMB * TEXTS, bytes_accessed=10 * 2**20, transcendentals=0
        ),
    )(*coeffs, *low)


def shards(pooled, w_img, text_emb, pos_index, log_scale, bias):
    z, xl, y, core = (lax.axis_index(a) for a in ("z", "xl", "y", "core"))
    scalars = jnp.stack([jnp.exp(log_scale[0]), bias[0]])
    pos = pos_index[0]
    lane = lax.broadcasted_iota(jnp.int32, (ROWS, PAD), 1)
    codes = jnp.where(lane == 0, (pos // 128)[:, None], jnp.where(lane == 1, (pos % 128)[:, None], 0))
    own = jnp.concatenate([pooled[0], codes.astype(BF)], axis=1)

    raw = text_emb[0].astype(F32)
    text_inv = lax.rsqrt(jnp.sum(raw * raw, axis=-1, keepdims=True) + 1e-06)
    text_unit = raw * text_inv
    plane = np.arange(NX * NY, dtype=np.int32)
    starts = lambda c: ((z * NX * NY + plane) * NC + c) * ROWS
    numbers = jnp.concatenate([starts(core), starts(1 - core), core[None]]).astype(jnp.int32)
    images, texts, scalars, numbers = gather(own, text_unit.astype(BF), scalars, numbers)

    first, second = images[:4], images[4:6]
    loss_a, coeffs_a, low_a, back_a = tile(scalars, numbers, first, w_img, texts)
    below, above, back_a = lax.optimization_barrier((images[5], images[6], back_a))
    last = [images[6], *gather_last(below, above)]
    loss_b, coeffs_b, low_b, back_b = tile(scalars, numbers, second, w_img, texts)
    early = (first + second, (back_a, back_b))
    loss_c, coeffs_c, low_c, w_mine, w_other = tile(scalars, numbers, last, w_img, texts, early)
    loss = jnp.concatenate([loss_a[0], loss_b[0], loss_c[0]])
    w = w_mine + flip(w_other, "core", NC).astype(F32)
    coeffs_c, w = lax.optimization_barrier((coeffs_c, w))
    t_mine, t_other = text_directions((coeffs_a, coeffs_b, coeffs_c), (low_a, low_b, low_c))
    t_sum = t_mine.astype(F32) + flip(t_other, "core", NC).astype(F32)
    blocks = t_sum.astype(BF).reshape(NX * NY, ROWS, D_EMB)
    weight_sum, losses, blocks = sum_weight(w, in_order(loss, z), blocks)
    text_dir = jnp.sum(blocks.astype(F32), axis=0)
    weight_grad = weight_sum / 64.0
    text_grad = (
        text_dir - text_unit * jnp.sum(text_unit * text_dir, axis=-1, keepdims=True)
    ) * text_inv
    row_loss = losses / (NX * NY * NZ * NC * ROWS)
    return row_loss[None], weight_grad, text_grad[None]


def solution(mesh):
    names = ("z", "xl", "y", "core", "rep")
    fine = Mesh(mesh.devices.reshape(NZ, NX, NY, NC, NR), names)
    blk = names[:4]
    return jax.shard_map(
        shards,
        mesh=fine,
        in_specs=(P("rep", blk, None), P(), P("rep", blk, None), P("rep", blk), P(), P()),
        out_specs=(P("rep", blk), P(names, None), P("rep", blk, None)),
        check_vma=False,
    )
```

```python
import functools

import jax
import jax.numpy as jnp
import numpy as np
from jax import lax
from jax.experimental import pallas as pl
from jax.experimental.pallas import tpu as pltpu
from jax.sharding import Mesh
from jax.sharding import PartitionSpec as P

NZ, NX, NY, NC, NR = 8, 2, 4, 2, 2
ROWS = 128
HALF = ROWS // 2
D_IMG = 1536
D_EMB = 1024
PAD = 128
IMGS = NZ * ROWS
TEXTS = NX * NY * NC * ROWS
STEP = 256
CHUNK = 512
BF, F32 = jnp.bfloat16, jnp.float32
Z_OFFSETS = (0, -1, 1, -2, 2, -3, 3, 4)


def shift(x, axis, n, by):
    return lax.ppermute(x, axis, [(i, (i + by) % n) for i in range(n)])


def flip(x, axis, n, bit=1):
    return lax.ppermute(x, axis, [(i, i ^ bit) for i in range(n)])


def exchange(x, axes):
    return lax.all_to_all(x, axes, 0, 0)


def gather(image, text, scalars, numbers):
    copies = jnp.broadcast_to(text, (NX * NY, *text.shape))
    near = exchange(copies, ("xl", "y")).reshape(NX * NY * ROWS, D_EMB)
    down, up = [image], [image]
    for k in range(3):
        down.append(shift(down[-1], "z", NZ, 1))
        up.append(shift(up[-1], "z", NZ, -1))
        if k == 1:
            down[-1], up[-1], near = lax.optimization_barrier((down[-1], up[-1], near))
        elif k == 0:
            tied = lax.optimization_barrier((down[-1], up[-1], scalars, numbers))
            down[-1], up[-1], scalars, numbers = tied
    images = [image, down[1], up[1], down[2], up[2], down[3], up[3]]
    return images, [near, flip(near, "core", NC)], scalars, numbers


def gather_last(below, above):
    return [shift(below[:HALF], "z", NZ, 1), shift(above[HALF:], "z", NZ, -1)]


def halve(w, dim, here, axis, n, bit, kind):
    mine = lax.dynamic_index_in_dim(w, here, dim, keepdims=False)
    other = lax.dynamic_index_in_dim(w, 1 - here, dim, keepdims=False)
    return mine + flip(other.astype(kind), axis, n, bit).astype(F32)


def halve_both(w, dim, losses, here, bit, kind):
    mine = lax.dynamic_index_in_dim(w, here, dim, keepdims=False)
    other = lax.dynamic_index_in_dim(w, 1 - here, dim, keepdims=False)
    mine_l = lax.dynamic_index_in_dim(losses, here, 0, keepdims=False)
    other_l = lax.dynamic_index_in_dim(losses, 1 - here, 0, keepdims=False).reshape(-1)
    if kind == BF:
        high = lax.reduce_precision(other_l, 8, 7)
        other_l = jnp.concatenate([high, other_l - high]).astype(BF)
    wide, n = w.shape[-1], other_l.shape[0]
    tail = jnp.pad(other_l, (0, 16 * wide - n)).reshape(16, wide)
    got = flip(jnp.concatenate([other.astype(kind).reshape(-1, wide), tail]), "z", NZ, bit)
    got_w = got[:-16].reshape(other.shape).astype(F32)
    got_l = got[-16:].reshape(-1)[:n].astype(F32).reshape(-1, *mine_l.shape)
    return mine + got_w, mine_l + jnp.sum(got_l, axis=0)


def sum_weight(w, losses, blocks):
    z, xl, y, core, rep = (lax.axis_index(a) for a in ("z", "xl", "y", "core", "rep"))
    w = w.reshape(2, 2, 2, NX, 2, 2, 24, D_EMB // 2)
    losses = losses.reshape(2, 2, 2, ROWS).transpose(2, 1, 0, 3)
    half = D_EMB // 4
    z_bits = z // 4, lax.rem(z // 2, 2), lax.rem(z, 2)
    a, b = w[..., :half], w[..., half:]
    a = halve(a, 2, z_bits[2], "z", NZ, 1, BF)
    b = halve(b, 4, y // 2, "y", NY, 2, BF)
    a = halve(a, 3, y // 2, "y", NY, 2, BF)
    b, losses = halve_both(b, 2, losses, z_bits[2], 1, BF)
    w = jnp.concatenate([a, b], axis=-1)
    blocks = exchange(blocks, ("xl", "y"))
    w = halve(w, 3, lax.rem(y, 2), "y", NY, 1, BF)
    w = halve(w, 2, xl, "xl", NX, 1, BF)
    w = halve(w.reshape(2, 2, NC, NR, 6, D_EMB // 2), 3, rep, "rep", NR, 1, F32)
    w, losses = halve_both(w, 1, losses, z_bits[1], 2, F32)
    w, losses = halve_both(w, 0, losses, z_bits[0], 4, F32)
    w, blocks = lax.optimization_barrier((w, blocks))
    own = lax.dynamic_index_in_dim(w, core, 0, keepdims=False)
    got = flip(lax.dynamic_index_in_dim(w, 1 - core, 0, keepdims=False), "core", NC)
    w = jnp.where(core == 0, jnp.concatenate([own, got], 1), jnp.concatenate([got, own], 1))
    return w, losses, blocks


def in_order(losses, z):
    at = {o: losses[i * ROWS : (i + 1) * ROWS] for i, o in enumerate(Z_OFFSETS)}
    ring = [at[o if o < 5 else o - NZ] for o in range(NZ)]
    return lax.dynamic_slice_in_dim(jnp.stack(ring + ring), NZ - z, NZ, 0)


NN = (((1,), (0,)), ((), ()))
NT = (((1,), (1,)), ((), ()))
TN = (((0,), (0,)), ((), ()))


def dot(a, b, dims, precision=None):
    return lax.dot_general(a, b, dims, precision=precision, preferred_element_type=F32)


def reciprocal(x):
    return pltpu.reciprocal(x, approx=True)


def pair_terms(products, hit, scale, shift_value):
    signed = jnp.where(hit, -scale, scale)
    e = jnp.exp(products * signed + jnp.where(hit, -shift_value, shift_value))
    u = 1.0 + e
    coeffs = (e * reciprocal(u) * signed).astype(BF)
    w = e.shape[1] // 4
    e4 = [e[:, k * w : (k + 1) * w] for k in range(4)]
    p = e4[0] + e4[1] * u[:, :w]
    q = e4[2] + e4[3] * u[:, 2 * w : 3 * w]
    g = p + q * (1.0 + p)
    v = 1.0 + g
    losses = jnp.log(v) + (g - (v - 1.0)) * reciprocal(v)
    return coeffs, losses


def fold(x):
    total = x[:, :128]
    for k in range(1, x.shape[1] // 128):
        total = total + x[:, k * 128 : (k + 1) * 128]
    return total


def tile_kernel(n_images, n_early, scalars, numbers, *refs):
    weigh = n_early > 0
    images, (w_img, *texts) = refs[:n_images], refs[n_images : n_images + 3]
    refs = refs[n_images + 3 :]
    if weigh:
        early, early_back, refs = refs[:n_early], refs[n_early : n_early + 2], refs[n_early + 2 :]
        loss, coeffs, low_out, w_mine, w_other, image, back = refs
    else:
        loss, coeffs, low_out, back_out, image = refs
    step = pl.program_id(0)
    scale, shift_value = scalars[0], scalars[1]

    @pl.when(step == 0)
    def _():
        at = 0
        for b in images:
            image[at : at + b.shape[0], :] = b[...]
            at += b.shape[0]

    rows = pl.ds(pl.multiple_of(step * STEP, STEP), STEP)
    codes = image[rows, D_IMG:].astype(F32)
    positive = (codes[:, 0:1] * 128.0 + codes[:, 1:2]).astype(jnp.int32)
    projected = dot(image[rows, :D_IMG], w_img[...], NN)
    inverse = lax.rsqrt(jnp.sum(projected * projected, axis=1, keepdims=True) + 1e-06)
    unit = projected * inverse
    low = unit.astype(BF)
    low_out[...] = low
    lane = lax.broadcasted_iota(jnp.int32, (1, ROWS), 1)
    chunks = [slice(k * CHUNK, (k + 1) * CHUNK) for k in range(TEXTS // CHUNK)]
    text = [t[k : k + CHUNK, :] for t in texts for k in range(0, t.shape[0], CHUNK)]
    products = dot(low, text[0], NT)
    direction = total = None
    for k, at in enumerate(chunks):
        here = products
        if k + 1 < len(chunks):
            products = dot(low, text[k + 1], NT)
        per = CHUNK // ROWS
        columns = jnp.concatenate([numbers[k * per + j] + lane for j in range(per)], axis=1)
        c, losses = pair_terms(here, positive == columns, scale, shift_value)
        coeffs[:, at] = c
        d = dot(c, text[k], NN)
        direction = d if direction is None else direction + d
        total = fold(losses) if total is None else total + fold(losses)
    loss[...] = dot(jnp.ones((8, 128), F32), total, NT, lax.Precision.HIGHEST)
    dots = jnp.sum(unit * direction, axis=1, keepdims=True)
    result = ((direction - unit * dots) * inverse).astype(BF)
    if not weigh:
        back_out[...] = result
        return
    back[rows, :] = result

    @pl.when(step == pl.num_programs(0) - 1)
    def _():
        core = numbers[NX * NY * NC]
        half = D_EMB // 2
        for ref, c in ((w_other, 1 - core), (w_mine, core)):
            columns = pl.ds(pl.multiple_of(c * half, half), half)
            for k in range(0, D_IMG, 512):
                at = slice(k, k + 512)
                w = dot(image[:, at], back[:, columns], TN)
                done = 0
                for part in early_back:
                    n = part.shape[0] // ROWS
                    left = jnp.concatenate([e[:, at] for e in early[done : done + n]])
                    w = w + dot(left, part[:, columns], TN)
                    done += n
                ref[k : k + 512, :] = w.astype(ref.dtype)


def tile(scalars, numbers, images, w_img, texts, early=None):
    def whole(x):
        return pl.BlockSpec(x.shape, lambda i: (0,) * len(x.shape), pipeline_mode=pl.Buffered(1))

    rows = lambda n: pl.BlockSpec((STEP, n), lambda i: (i, 0))
    smem = pl.BlockSpec(memory_space=pltpu.SMEM)
    half = sum(b.shape[0] for b in images)
    out_shape = [
        jax.ShapeDtypeStruct((8, half), F32),
        jax.ShapeDtypeStruct((half, TEXTS), BF),
        jax.ShapeDtypeStruct((half, D_EMB), BF),
    ]
    out_specs = [pl.BlockSpec((8, STEP), lambda i: (0, i)), rows(TEXTS), rows(D_EMB)]
    scratch = [pltpu.VMEM((half, D_IMG + PAD), BF)]
    arrays = [*images, w_img, *texts]
    flops = 2 * half * D_EMB * (2 * TEXTS + D_IMG)
    if early is None:
        out_shape += [jax.ShapeDtypeStruct((half, D_EMB), BF)]
        out_specs += [rows(D_EMB)]
    else:
        arrays += [*early[0], *early[1]]
        out_shape += [
            jax.ShapeDtypeStruct((D_IMG, D_EMB // 2), F32),
            jax.ShapeDtypeStruct((D_IMG, D_EMB // 2), BF),
        ]
        out_specs += [whole(out_shape[3]), whole(out_shape[4])]
        scratch += [pltpu.VMEM((half, D_EMB), BF)]
        flops += 2 * IMGS * D_EMB * D_IMG
    return pl.pallas_call(
        functools.partial(tile_kernel, len(images), len(early[0]) if early else 0),
        grid=(half // STEP,),
        in_specs=[smem, smem] + [whole(a) for a in arrays],
        out_specs=out_specs,
        out_shape=out_shape,
        scratch_shapes=scratch,
        compiler_params=pltpu.CompilerParams(vmem_limit_bytes=56 * 2**20),
        cost_estimate=pl.CostEstimate(
            flops=flops, bytes_accessed=16 * 2**20, transcendentals=2 * half * TEXTS
        ),
    )(scalars, numbers, *arrays)


def text_kernel(*refs):
    coeffs, low, (mine, other) = refs[:3], refs[3:6], refs[6:]
    total = sum(dot(c[...], v[...], TN) for c, v in zip(coeffs, low))
    step, half = pl.program_id(0), pl.num_programs(0) // 2

    @pl.when(step < half)
    def _():
        other[...] = total.astype(BF)

    @pl.when(step >= half)
    def _():
        mine[...] = total.astype(BF)


def text_directions(coeffs, low):
    block = 256
    steps = TEXTS // block // 2
    column = lambda c: pl.BlockSpec((c.shape[0], block), lambda i: (0, (i + steps) % (2 * steps)))
    keep = lambda v: pl.BlockSpec(v.shape, lambda i: (0, 0), pipeline_mode=pl.Buffered(1))
    return pl.pallas_call(
        text_kernel,
        grid=(TEXTS // block,),
        in_specs=[*map(column, coeffs), *map(keep, low)],
        out_specs=[
            pl.BlockSpec((block, D_EMB), lambda i: (jnp.maximum(i - steps, 0), 0)),
            pl.BlockSpec((block, D_EMB), lambda i: (jnp.minimum(i, steps - 1), 0)),
        ],
        out_shape=[jax.ShapeDtypeStruct((TEXTS // 2, D_EMB), BF)] * 2,
        compiler_params=pltpu.CompilerParams(vmem_limit_bytes=60 * 2**20),
        cost_estimate=pl.CostEstimate(
            flops=2 * IMGS * D_EMB * TEXTS, bytes_accessed=10 * 2**20, transcendentals=0
        ),
    )(*coeffs, *low)


def shards(pooled, w_img, text_emb, pos_index, log_scale, bias):
    z, xl, y, core = (lax.axis_index(a) for a in ("z", "xl", "y", "core"))
    scalars = jnp.stack([jnp.exp(log_scale[0]), bias[0]])
    pos = pos_index[0]
    lane = lax.broadcasted_iota(jnp.int32, (ROWS, PAD), 1)
    codes = jnp.where(lane == 0, (pos // 128)[:, None], jnp.where(lane == 1, (pos % 128)[:, None], 0))
    own = jnp.concatenate([pooled[0], codes.astype(BF)], axis=1)

    raw = text_emb[0].astype(F32)
    text_inv = lax.rsqrt(jnp.sum(raw * raw, axis=-1, keepdims=True) + 1e-06)
    text_unit = raw * text_inv
    plane = np.arange(NX * NY, dtype=np.int32)
    starts = lambda c: ((z * NX * NY + plane) * NC + c) * ROWS
    numbers = jnp.concatenate([starts(core), starts(1 - core), core[None]]).astype(jnp.int32)
    images, texts, scalars, numbers = gather(own, text_unit.astype(BF), scalars, numbers)

    first, second = images[:4], images[4:6]
    loss_a, coeffs_a, low_a, back_a = tile(scalars, numbers, first, w_img, texts)
    below, above, back_a = lax.optimization_barrier((images[5], images[6], back_a))
    last = [images[6], *gather_last(below, above)]
    loss_b, coeffs_b, low_b, back_b = tile(scalars, numbers, second, w_img, texts)
    early = (first + second, (back_a, back_b))
    loss_c, coeffs_c, low_c, w_mine, w_other = tile(scalars, numbers, last, w_img, texts, early)
    loss = jnp.concatenate([loss_a[0], loss_b[0], loss_c[0]])
    w = w_mine + flip(w_other, "core", NC).astype(F32)
    coeffs_c, w = lax.optimization_barrier((coeffs_c, w))
    t_mine, t_other = text_directions((coeffs_a, coeffs_b, coeffs_c), (low_a, low_b, low_c))
    t_sum = t_mine.astype(F32) + flip(t_other, "core", NC).astype(F32)
    blocks = t_sum.astype(BF).reshape(NX * NY, ROWS, D_EMB)
    weight_sum, losses, blocks = sum_weight(w, in_order(loss, z), blocks)
    text_dir = jnp.sum(blocks.astype(F32), axis=0)
    weight_grad = weight_sum / 64.0
    text_grad = (
        text_dir - text_unit * jnp.sum(text_unit * text_dir, axis=-1, keepdims=True)
    ) * text_inv
    row_loss = losses / (NX * NY * NZ * NC * ROWS)
    return row_loss[None], weight_grad, text_grad[None]


def solution(mesh):
    names = ("z", "xl", "y", "core", "rep")
    fine = Mesh(mesh.devices.reshape(NZ, NX, NY, NC, NR), names)
    blk = names[:4]
    return jax.shard_map(
        shards,
        mesh=fine,
        in_specs=(P("rep", blk, None), P(), P("rep", blk, None), P("rep", blk), P(), P()),
        out_specs=(P("rep", blk), P(names, None), P("rep", blk, None)),
        check_vma=False,
    )
```
